256 devices in a mesh: row: 4 (over y), col: 2 (over z_lo), depth: 32 (over z_hi, x, core).
Axes of the slice: x: 4, y: 4, z: 8 (z_hi: 4, z_lo: 2; z = z_hi * 2 + z_lo), core: 2. Of those that a mesh axis runs over, the one named last changes fastest.
Arguments:
- inputs: bfloat16 [1024, 12288], P(('col', 'depth'), 'row'), may hold values from -6 to 6
- weight: bfloat16 [12288, 49152], P('row', ('col', 'depth')), may hold values from -0.0546875 to 0.0546875
- out_grad: bfloat16 [1024, 49152], P('row', ('col', 'depth')), may hold values from -16 to 16
Outputs:
- activated: bfloat16 [1024, 49152], P('row', ('col', 'depth'))
- input_grad: bfloat16 [1024, 12288], P(('col', 'depth'), 'row')
- weight_grad: bfloat16 [12288, 49152], P('row', ('col', 'depth'))
The draws below stay inside these ranges and needn't reach their ends.
All inputs are finite; a program needn't handle non-finite values.
Results may differ from the reference program's by a relative error of at most 0.0049.
Values may be sent and summed in bfloat16 or wider, within the bound.
No kernel may reach another device: no remote copies, remote signals or barrier semaphores. Data moves between devices by JAX's collectives and lax.ppermute only.
A program may use at most 128 MiB of HBM per device.

```python
import math
import jax
import jax.numpy as jnp
from jax import lax

D = 12288
FF = 49152
TOKENS = 1024


def strengthened(result, stream_key, source, target, shards_of, factor):
    def block_of(dim):
        return (jnp.arange(result.shape[dim]) // (result.shape[dim] // shards_of)).reshape((-1,) + (1,) * (result.ndim - 1 - dim))

    near = jax.random.permutation(stream_key, shards_of)[block_of(target)]
    other_side = (block_of(target) + shards_of // 2) % shards_of
    return jnp.where((block_of(source) == near) | (block_of(source) == other_side), factor * result, result)


def level_of(own_key, dims, cuts, least, top_value):
    def one(position, parts):
        steps = jax.random.uniform(jax.random.fold_in(jax.random.fold_in(own_key, 6), position), (parts,), jnp.float32, least / len(cuts), top_value / len(cuts))
        return jnp.repeat(jnp.exp(steps), dims[position] // parts).reshape((-1,) + (1,) * (len(dims) - position - 1))

    level = one(*cuts[0])
    for cut in cuts[1:]:
        level = level * one(*cut)
    return level


def bell_draw(stream_key, shape, scale, bound, shards=(), kind=jnp.bfloat16):
    loudness = level_of(stream_key, shape, shards, -0.22, 0.18) if shards else 1.0
    drawn = jax.random.normal(stream_key, shape, jnp.float32) * scale * loudness
    return jnp.minimum(jnp.maximum(drawn, -bound), bound).astype(kind)


def bell_draw_with(rng, dims, scale, bound, shards, heavy, dtype=jnp.bfloat16):
    entries = scale * jax.random.normal(rng, dims, jnp.float32)
    if shards:
        entries = entries * level_of(rng, dims, shards, -0.22, 0.18)
    return jnp.clip(strengthened(entries, jax.random.fold_in(rng, 3), *heavy), -bound, bound).astype(dtype)


def setup_inputs(seed: int = 0) -> dict:
    seeds = jax.random.split(jax.random.key(seed), 4)
    inputs = bell_draw(seeds[0], (TOKENS, D), 1.0, 6.0, ((0, 64), (1, 4)))
    weight = bell_draw(seeds[1], (D, FF), D ** -0.5, 0.0546875, ((0, 4), (1, 64)))
    out_grad = bell_draw_with(seeds[2], (TOKENS, FF), 1.0, 16.0, ((0, 4), (1, 64)), (1, 0, 64, 4.0))
    return dict(inputs=inputs, weight=weight, out_grad=out_grad)


gelu_coef = 0.044715

def reference(inputs, weight, out_grad):
    pre = jnp.dot(inputs, weight, preferred_element_type=jnp.float32)
    scale = math.sqrt(2.0 / math.pi)
    inner = scale * (pre + gelu_coef * pre * pre * pre)
    tanh_val = jnp.tanh(inner)
    activated = (0.5 * pre * (1.0 + tanh_val)).astype(jnp.bfloat16)
    slope = 0.5 * (1.0 + tanh_val) + 0.5 * pre * (1.0 - tanh_val * tanh_val) * scale * (1.0 + 3.0 * gelu_coef * pre * pre)
    pre_grad = (out_grad.astype(jnp.float32) * slope).astype(jnp.bfloat16)
    input_grad = lax.dot_general(pre_grad, weight, (((1,), (1,)), ((), ())), preferred_element_type=jnp.float32).astype(jnp.bfloat16)
    weight_grad = lax.dot_general(inputs, pre_grad, (((0,), (0,)), ((), ())), preferred_element_type=jnp.float32).astype(jnp.bfloat16)
    return (activated, input_grad, weight_grad)
```

```python
import functools
import math

import jax
import jax.numpy as jnp
import numpy as np
from jax import lax
from jax.experimental import pallas as pl
from jax.experimental.pallas import tpu as pltpu
from jax.sharding import Mesh
from jax.sharding import PartitionSpec as P

gelu_coef = 0.044715

AXES = ("y", "zl", "zh", "x", "core")
SIZES = (4, 2, 4, 4, 2)
Z = ("zl", "zh")
BF = jnp.bfloat16
F32 = jnp.float32


def permute(array, move):
    pairs = []
    for y, zl, zh, x, core in np.ndindex(*SIZES):
        y2, x2, core2 = move(y, x, core)
        source = np.ravel_multi_index((y, zl, zh, x, core), SIZES)
        target = np.ravel_multi_index((y2, zl, zh, x2, core2), SIZES)
        pairs.append((int(source), int(target)))
    return lax.ppermute(array, AXES, pairs)


first = lambda core: 3 if core else 1
second = lambda core: 1 if core else 3
swap_core = lambda y, x, core: (y, x, 1 - core)
x_first = lambda y, x, core: (y, x ^ first(core), core)
x_second = lambda y, x, core: (y, x ^ second(core), core)
y_first = lambda y, x, core: (y ^ first(core), x, core)
y_second = lambda y, x, core: (y ^ second(core), x, core)


def gelu_pair(pre, cotangent):
    scale = math.sqrt(2.0 / math.pi)
    inner = scale * (pre + gelu_coef * pre * pre * pre)
    tanh_val = jnp.tanh(inner)
    activated = (0.5 * pre * (1.0 + tanh_val)).astype(BF)
    slope = 0.5 * (1.0 + tanh_val) + 0.5 * pre * (1.0 - tanh_val * tanh_val) * scale * (
        1.0 + 3.0 * gelu_coef * pre * pre
    )
    return activated, (cotangent.astype(F32) * slope).astype(BF)


def gelu_kernel(place_ref, own_ref, other_ref, cot_ref, act_ref, grad_ref):
    pre = own_ref[0] + other_ref[0].astype(F32)
    activated, grad = gelu_pair(pre, cot_ref[:, 0])
    act_ref[:, 0] = activated
    grad_ref[0] = grad


def gelu_call(place, own, other, cotangent):
    slots, two, t, f = own.shape
    local = pl.BlockSpec((1, two, t, f), lambda s, place: (s, 0, 0, 0))
    placed = pl.BlockSpec((two, 1, t, f), lambda s, place: (0, place[s], 0, 0))
    return pl.pallas_call(
        gelu_kernel,
        grid_spec=pltpu.PrefetchScalarGridSpec(
            num_scalar_prefetch=1,
            grid=(slots,),
            in_specs=[local, local, placed],
            out_specs=[placed, local],
        ),
        out_shape=[
            jax.ShapeDtypeStruct(cotangent.shape, BF),
            jax.ShapeDtypeStruct(own.shape, BF),
        ],
        cost_estimate=pl.CostEstimate(flops=30 * own.size, bytes_accessed=12 * own.size, transcendentals=own.size),
        name="gelu",
    )(place, own, other, cotangent)


def order_kernel(place_ref, a_ref, b_ref, c_ref, out_ref):
    out_ref[:, pl.ds(place_ref[0], 1)] = a_ref[...][:, None]
    out_ref[:, pl.ds(place_ref[1], 1)] = b_ref[...][:, None]
    out_ref[:, pl.ds(place_ref[2], 1)] = c_ref[0][:, None]
    out_ref[:, pl.ds(place_ref[3], 1)] = c_ref[1][:, None]


def order_call(place, a, b, c):
    slots, rows, f = a.shape
    whole = pl.BlockSpec(memory_space=pltpu.VMEM)
    return pl.pallas_call(
        order_kernel,
        in_specs=[pl.BlockSpec(memory_space=pltpu.SMEM), whole, whole, whole],
        out_specs=whole,
        out_shape=jax.ShapeDtypeStruct((slots, 4, rows, f), BF),
        compiler_params=pltpu.CompilerParams(vmem_limit_bytes=16 * 2**20),
        cost_estimate=pl.CostEstimate(flops=0, bytes_accessed=16 * a.size, transcendentals=0),
        name="order",
    )(place, a, b, c)


def body(inputs, weight, out_grad):
    y, x, core = lax.axis_index("y"), lax.axis_index("x"), lax.axis_index("core")
    t, d = inputs.shape
    f = weight.shape[1]
    near = jnp.where(core == 0, 1, 3)
    far = jnp.where(core == 0, 3, 1)
    pick = lambda a, i: lax.dynamic_index_in_dim(a, i, 1, keepdims=False)

    own = lax.all_to_all(jnp.broadcast_to(inputs[None], (8, t, d)), Z, 0, 0, tiled=True)
    one = permute(own, x_first)
    two = permute(own, x_second)
    three = permute(one, x_second)
    o0, o1, o2, o3 = (permute(p, swap_core) for p in (own, one, two, three))
    tokens = jnp.concatenate([own, o0, one, o2, two, o1, three, o3], 0).reshape(64 * t, d)

    part = jnp.dot(tokens, weight, preferred_element_type=F32).reshape(8, 4, 2 * t, f)
    send = jnp.stack([pick(part, y ^ near), pick(part, y ^ 2)]).astype(BF)
    got = permute(send, y_first).astype(F32)
    mine = pick(part, y) + got[0]
    theirs = pick(part, y ^ far) + got[1]
    got = permute(theirs.astype(BF), y_second)

    steps = jnp.stack([jnp.int32(0), near, far, jnp.int32(2)]).astype(jnp.int32)
    place = ((x ^ steps)[:, None] * 2 + (core ^ jnp.arange(2, dtype=jnp.int32))[None]).reshape(8).astype(jnp.int32)
    activated, grad = gelu_call(
        place, mine.reshape(8, 2, t, f), got.reshape(8, 2, t, f), out_grad.reshape(2, 8, t, f)
    )

    grad = grad.reshape(8, 2 * t, f)
    other = permute(grad, y_second)
    rest = permute(jnp.stack([grad, other]), y_first)
    order = jnp.stack([y, y ^ far, y ^ near, y ^ 2]).astype(jnp.int32)
    grad_all = order_call(order, grad, other, rest).reshape(64 * t, f)

    part = lax.dot_general(grad_all, weight, (((1,), (1,)), ((), ())), preferred_element_type=F32)
    part = part.reshape(4, 2, 8 * t, d)
    got = permute(part[:, 1].astype(BF), swap_core)
    total = part[:, 0] + jnp.stack([got[0], got[2], got[1], got[3]]).astype(F32)
    got = permute(total[2:].astype(BF), x_second)
    total = total[:2] + got.astype(F32)
    got = permute(total[1].astype(BF), x_first)
    total = (total[0] + got.astype(F32)).astype(BF)
    blocks = lax.all_to_all(total.reshape(8, t, d), Z, 0, 0, tiled=True)
    input_grad = jnp.sum(blocks.astype(F32), 0).astype(BF)

    weight_grad = lax.dot_general(tokens, grad_all, (((0,), (0,)), ((), ())), preferred_element_type=F32).astype(BF)
    return activated.reshape(16 * t, f), input_grad, weight_grad


def solution(mesh):
    fine = Mesh(mesh.devices.reshape(SIZES), AXES)
    tokens = ("zl", "zh", "x", "core")
    specs = (P(tokens, "y"), P("y", tokens), P("y", tokens))
    return jax.shard_map(
        body, mesh=fine, in_specs=specs, out_specs=(specs[1], specs[0], specs[1]), check_vma=False
    )
```

```python
import functools
import math

import jax
import jax.numpy as jnp
import numpy as np
from jax import lax
from jax.experimental import pallas as pl
from jax.experimental.pallas import tpu as pltpu
from jax.sharding import Mesh
from jax.sharding import PartitionSpec as P

gelu_coef = 0.044715

AXES = ("y", "zl", "zh", "x", "core")
SIZES = (4, 2, 4, 4, 2)
Z = ("zl", "zh")
BF = jnp.bfloat16
F32 = jnp.float32


def permute(array, move):
    pairs = []
    for y, zl, zh, x, core in np.ndindex(*SIZES):
        y2, x2, core2 = move(y, x, core)
        source = np.ravel_multi_index((y, zl, zh, x, core), SIZES)
        target = np.ravel_multi_index((y2, zl, zh, x2, core2), SIZES)
        pairs.append((int(source), int(target)))
    return lax.ppermute(array, AXES, pairs)


first = lambda core: 3 if core else 1
second = lambda core: 1 if core else 3
swap_core = lambda y, x, core: (y, x, 1 - core)
x_first = lambda y, x, core: (y, x ^ first(core), core)
x_second = lambda y, x, core: (y, x ^ second(core), core)
y_first = lambda y, x, core: (y ^ first(core), x, core)
y_second = lambda y, x, core: (y ^ second(core), x, core)


def gelu_pair(pre, cotangent):
    scale = math.sqrt(2.0 / math.pi)
    inner = scale * (pre + gelu_coef * pre * pre * pre)
    tanh_val = jnp.tanh(inner)
    activated = (0.5 * pre * (1.0 + tanh_val)).astype(BF)
    slope = 0.5 * (1.0 + tanh_val) + 0.5 * pre * (1.0 - tanh_val * tanh_val) * scale * (
        1.0 + 3.0 * gelu_coef * pre * pre
    )
    return activated, (cotangent.astype(F32) * slope).astype(BF)


def gelu_kernel(place_ref, own_ref, other_ref, cot_ref, act_ref, grad_ref):
    for slot in range(own_ref.shape[0]):
        pre = own_ref[slot] + other_ref[slot].astype(F32)
        activated, grad = gelu_pair(pre, cot_ref[place_ref[slot]])
        act_ref[place_ref[slot]] = activated
        grad_ref[slot] = grad


def gelu_call(place, own, other, cotangent):
    whole = pl.BlockSpec(memory_space=pltpu.VMEM)
    return pl.pallas_call(
        gelu_kernel,
        in_specs=[pl.BlockSpec(memory_space=pltpu.SMEM), whole, whole, whole],
        out_specs=[whole, whole],
        out_shape=[jax.ShapeDtypeStruct(own.shape, BF)] * 2,
        compiler_params=pltpu.CompilerParams(vmem_limit_bytes=16 * 2**20),
        cost_estimate=pl.CostEstimate(flops=30 * own.size, bytes_accessed=12 * own.size, transcendentals=own.size),
        name="gelu",
    )(place, own, other, cotangent)


def order_kernel(place_ref, a_ref, b_ref, c_ref, out_ref):
    out_ref[:, pl.ds(place_ref[0], 1)] = a_ref[...][:, None]
    out_ref[:, pl.ds(place_ref[1], 1)] = b_ref[...][:, None]
    out_ref[:, pl.ds(place_ref[2], 1)] = c_ref[0][:, None]
    out_ref[:, pl.ds(place_ref[3], 1)] = c_ref[1][:, None]


def order_call(place, a, b, c):
    slots, rows, f = a.shape
    whole = pl.BlockSpec(memory_space=pltpu.VMEM)
    return pl.pallas_call(
        order_kernel,
        in_specs=[pl.BlockSpec(memory_space=pltpu.SMEM), whole, whole, whole],
        out_specs=whole,
        out_shape=jax.ShapeDtypeStruct((slots, 4, rows, f), BF),
        compiler_params=pltpu.CompilerParams(vmem_limit_bytes=16 * 2**20),
        cost_estimate=pl.CostEstimate(flops=0, bytes_accessed=16 * a.size, transcendentals=0),
        name="order",
    )(place, a, b, c)


CHUNKS = 2


def after(value, *others):
    return lax.optimization_barrier((value, *others))[0]


class Chunk:
    pass


def body(inputs, weight, out_grad):
    y, x, core = lax.axis_index("y"), lax.axis_index("x"), lax.axis_index("core")
    d, f = weight.shape
    t = inputs.shape[0] // CHUNKS
    near = jnp.where(core == 0, 1, 3)
    far = jnp.where(core == 0, 3, 1)
    pick = lambda a, i: lax.dynamic_index_in_dim(a, i, 1, keepdims=False)

    steps = jnp.stack([jnp.int32(0), near, far, jnp.int32(2)]).astype(jnp.int32)
    place = ((x ^ steps)[None] * 2 + (core ^ jnp.arange(2, dtype=jnp.int32))[:, None]).reshape(8).astype(jnp.int32)
    order = jnp.stack([y, y ^ far, y ^ near, y ^ 2]).astype(jnp.int32)
    cotangents = jnp.transpose(out_grad.reshape(2, 8, CHUNKS, t, f), (2, 1, 0, 3, 4)).reshape(CHUNKS, 8, 2 * t, f)

    def spread(c, block):
        c.own = lax.all_to_all(jnp.broadcast_to(block[None], (8, t, d)), Z, 0, 0, tiled=True)

    def along_x(c, *wait):
        source = after(c.own, *wait) if wait else c.own
        c.one = permute(source, x_first)
        c.two = permute(source, x_second)
        c.three = permute(c.one, x_second)

    def assemble(c):
        c.other = [permute(p, swap_core) for p in (c.own, c.two, c.one, c.three)]
        c.tokens = jnp.concatenate([c.own, c.one, c.two, c.three] + c.other, 0).reshape(64 * t, d)

    def project(c, *wait):
        tokens = after(c.tokens, *wait) if wait else c.tokens
        c.part = jnp.dot(tokens, weight, preferred_element_type=F32).reshape(8, 4, 2 * t, f)
        c.send = jnp.stack([pick(c.part, y ^ near), pick(c.part, y ^ 2)]).astype(BF)

    def sum_first(c):
        got = permute(c.send, y_first).astype(F32)
        c.mine = pick(c.part, y) + got[0]
        c.theirs = (pick(c.part, y ^ far) + got[1]).astype(BF)

    def sum_second(c):
        c.got = permute(c.theirs, y_second)

    def gelu(c, cotangent, *wait):
        got = after(c.got, *wait) if wait else c.got
        c.activated, c.grad = gelu_call(place, c.mine, got, cotangent)

    def spread_first(c):
        c.grad_far = permute(c.grad, y_second)

    def spread_second(c, wait=(), behind=()):
        rest = permute(after(jnp.stack([c.grad, c.grad_far]), *wait), y_first)
        c.grad_all = order_call(order, c.grad, c.grad_far, after(rest, *behind)).reshape(2, 32 * t, f)

    def back(c, *wait):
        dims = (((1,), (1,)), ((), ()))
        give = lax.dot_general(c.grad_all[1], weight, dims, preferred_element_type=F32).astype(BF)
        keep = lax.dot_general(c.grad_all[0], weight, dims, preferred_element_type=F32).reshape(4, 8 * t, d)
        got = permute(give.reshape(4, 8 * t, d), swap_core)
        c.away = (keep[2:] + jnp.stack([got[1], got[3]]).astype(F32)).astype(BF)
        c.here = keep[:2] + jnp.stack([got[0], got[2]]).astype(F32)

    def reduce_first(c, wait=(), behind=()):
        got = after(permute(after(c.away, *wait), x_second), *behind).astype(F32)
        c.away = (c.here[1] + got[1]).astype(BF)
        c.here = c.here[0] + got[0]

    def reduce_second(c, *wait):
        got = permute(after(c.away, *wait) if wait else c.away, x_first).astype(F32)
        c.total = (c.here + got).astype(BF).reshape(8, t, d)

    def reduce_last(c, *wait):
        total = after(c.total, *wait) if wait else c.total
        blocks = lax.all_to_all(total, Z, 0, 0, tiled=True)
        c.input_grad = jnp.sum(blocks.astype(F32), 0).astype(BF)

    def weights(c, *wait):
        grads = after(c.grad_all, *wait).reshape(64 * t, f)
        return lax.dot_general(c.tokens, grads, (((0,), (0,)), ((), ())), preferred_element_type=F32)

    a, b = Chunk(), Chunk()
    spread(a, inputs[:t])
    along_x(a)
    spread(b, after(inputs[t:], a.own))
    assemble(a)
    along_x(b, a.three)
    project(a)
    sum_first(a)
    sum_second(a)
    assemble(b)
    project(b, a.theirs)
    gelu(a, cotangents[0])
    spread_first(a)
    sum_first(b)
    spread_second(a)
    sum_second(b)
    gelu(b, cotangents[1], a.grad_far)
    back(a)
    spread_first(b)
    wa = weights(a, a.away)
    sent = a.away
    reduce_first(a)
    spread_second(b, wait=(sent,), behind=(wa,))
    back(b)
    sent = a.away
    reduce_second(a)
    wb = weights(b, b.away, a.total)
    weight_grad = (wa + wb).astype(BF)
    reduce_first(b, wait=(sent,), behind=(weight_grad,))
    reduce_last(a)
    reduce_second(b)
    reduce_last(b)

    input_grad = jnp.concatenate([a.input_grad, b.input_grad], 0)
    activated = jnp.stack([after(a.activated, b.total), b.activated]).reshape(CHUNKS, 8, 2, t, f)
    activated = jnp.transpose(activated, (2, 1, 0, 3, 4)).reshape(out_grad.shape)
    return activated, input_grad, weight_grad


def solution(mesh):
    fine = Mesh(mesh.devices.reshape(SIZES), AXES)
    tokens = ("zl", "zh", "x", "core")
    specs = (P(tokens, "y"), P("y", tokens), P("y", tokens))
    return jax.shard_map(
        body, mesh=fine, in_specs=specs, out_specs=(specs[1], specs[0], specs[1]), check_vma=False
    )
```

```python
import functools
import math

import jax
import jax.numpy as jnp
import numpy as np
from jax import lax
from jax.experimental import pallas as pl
from jax.experimental.pallas import tpu as pltpu
from jax.sharding import Mesh
from jax.sharding import PartitionSpec as P

gelu_coef = 0.044715

AXES = ("y", "zl", "zh", "x", "core")
SIZES = (4, 2, 4, 4, 2)
Z = ("zl", "zh")
BF = jnp.bfloat16
F32 = jnp.float32


def permute(array, move):
    pairs = []
    for y, zl, zh, x, core in np.ndindex(*SIZES):
        y2, x2, core2 = move(y, x, core)
        source = np.ravel_multi_index((y, zl, zh, x, core), SIZES)
        target = np.ravel_multi_index((y2, zl, zh, x2, core2), SIZES)
        pairs.append((int(source), int(target)))
    return lax.ppermute(array, AXES, pairs)


first = lambda core: 3 if core else 1
second = lambda core: 1 if core else 3
swap_core = lambda y, x, core: (y, x, 1 - core)
x_first = lambda y, x, core: (y, x ^ first(core), core)
x_second = lambda y, x, core: (y, x ^ second(core), core)
y_first = lambda y, x, core: (y ^ first(core), x, core)
y_second = lambda y, x, core: (y ^ second(core), x, core)


def gelu_pair(pre, cotangent):
    scale = math.sqrt(2.0 / math.pi)
    inner = scale * (pre + gelu_coef * pre * pre * pre)
    tanh_val = jnp.tanh(inner)
    activated = (0.5 * pre * (1.0 + tanh_val)).astype(BF)
    slope = 0.5 * (1.0 + tanh_val) + 0.5 * pre * (1.0 - tanh_val * tanh_val) * scale * (
        1.0 + 3.0 * gelu_coef * pre * pre
    )
    return activated, (cotangent.astype(F32) * slope).astype(BF)


def gelu_kernel(place_ref, own_ref, other_ref, cot_ref, act_ref, grad_ref):
    for slot in range(own_ref.shape[0]):
        pre = own_ref[slot] + other_ref[slot].astype(F32)
        activated, grad = gelu_pair(pre, cot_ref[place_ref[slot]])
        act_ref[place_ref[slot]] = activated
        grad_ref[slot] = grad


def gelu_call(place, own, other, cotangent):
    whole = pl.BlockSpec(memory_space=pltpu.VMEM)
    return pl.pallas_call(
        gelu_kernel,
        in_specs=[pl.BlockSpec(memory_space=pltpu.SMEM), whole, whole, whole],
        out_specs=[whole, whole],
        out_shape=[jax.ShapeDtypeStruct(own.shape, BF)] * 2,
        compiler_params=pltpu.CompilerParams(vmem_limit_bytes=16 * 2**20),
        cost_estimate=pl.CostEstimate(flops=30 * own.size, bytes_accessed=12 * own.size, transcendentals=own.size),
        name="gelu",
    )(place, own, other, cotangent)


def order_kernel(place_ref, a_ref, b_ref, c_ref, out_ref):
    out_ref[:, pl.ds(place_ref[0], 1)] = a_ref[...][:, None]
    out_ref[:, pl.ds(place_ref[1], 1)] = b_ref[...][:, None]
    out_ref[:, pl.ds(place_ref[2], 1)] = c_ref[0][:, None]
    out_ref[:, pl.ds(place_ref[3], 1)] = c_ref[1][:, None]


def order_call(place, a, b, c):
    slots, rows, f = a.shape
    whole = pl.BlockSpec(memory_space=pltpu.VMEM)
    return pl.pallas_call(
        order_kernel,
        in_specs=[pl.BlockSpec(memory_space=pltpu.SMEM), whole, whole, whole],
        out_specs=whole,
        out_shape=jax.ShapeDtypeStruct((slots, 4, rows, f), BF),
        compiler_params=pltpu.CompilerParams(vmem_limit_bytes=16 * 2**20),
        cost_estimate=pl.CostEstimate(flops=0, bytes_accessed=16 * a.size, transcendentals=0),
        name="order",
    )(place, a, b, c)


CHUNKS = 2


def after(value, *others):
    return lax.optimization_barrier((value, *others))[0] if others else value


class Chunk:
    pass


def body(inputs, weight, out_grad):
    y, x, core = lax.axis_index("y"), lax.axis_index("x"), lax.axis_index("core")
    d, f = weight.shape
    t = inputs.shape[0] // CHUNKS
    near = jnp.where(core == 0, 1, 3)
    far = jnp.where(core == 0, 3, 1)
    pick = lambda a, i: lax.dynamic_index_in_dim(a, i, 1, keepdims=False)

    steps = jnp.stack([jnp.int32(0), near, far, jnp.int32(2)]).astype(jnp.int32)
    place = ((x ^ steps)[None] * 2 + (core ^ jnp.arange(2, dtype=jnp.int32))[:, None]).reshape(8).astype(jnp.int32)
    order = jnp.stack([y, y ^ far, y ^ near, y ^ 2]).astype(jnp.int32)
    cotangents = jnp.transpose(out_grad.reshape(2, 8, CHUNKS, t, f), (2, 1, 0, 3, 4)).reshape(CHUNKS, 8, 2 * t, f)

    def spread(c, block, *wait):
        copies = after(jnp.broadcast_to(block[None], (8, t, d)), *wait)
        c.own = lax.all_to_all(copies, Z, 0, 0, tiled=True)

    def along_x(c, *wait):
        source = after(c.own, *wait) if wait else c.own
        c.one = permute(source, x_first)
        c.two = permute(source, x_second)
        c.three = permute(c.one, x_second)

    def assemble(c):
        c.other = [permute(p, swap_core) for p in (c.own, c.two, c.one, c.three)]
        c.tokens = jnp.concatenate([c.own, c.one, c.two, c.three] + c.other, 0).reshape(64 * t, d)

    def project(c, *wait):
        tokens = after(c.tokens, *wait) if wait else c.tokens
        c.part = jnp.dot(tokens, weight, preferred_element_type=F32).reshape(8, 4, 2 * t, f)
        c.send = jnp.stack([pick(c.part, y ^ near), pick(c.part, y ^ 2)]).astype(BF)

    def sum_first(c):
        got = permute(c.send, y_first).astype(F32)
        c.mine = pick(c.part, y) + got[0]
        c.theirs = (pick(c.part, y ^ far) + got[1]).astype(BF)

    def sum_second(c):
        c.got = permute(c.theirs, y_second)

    def gelu(c, cotangent, *wait):
        got = after(c.got, *wait) if wait else c.got
        c.activated, c.grad = gelu_call(place, c.mine, got, cotangent)

    def spread_first(c):
        c.grad_far = permute(c.grad, y_second)

    def spread_second(c, wait=(), behind=()):
        rest = permute(after(jnp.stack([c.grad, c.grad_far]), *wait), y_first)
        c.grad_all = order_call(order, c.grad, c.grad_far, after(rest, *behind)).reshape(2, 32 * t, f)

    def back(c, *wait):
        dims = (((1,), (1,)), ((), ()))
        give = lax.dot_general(c.grad_all[1], weight, dims, preferred_element_type=F32).astype(BF)
        keep = lax.dot_general(c.grad_all[0], weight, dims, preferred_element_type=F32).reshape(4, 8 * t, d)
        got = permute(give.reshape(4, 8 * t, d), swap_core)
        c.away = (keep[2:] + jnp.stack([got[1], got[3]]).astype(F32)).astype(BF)
        c.here = keep[:2] + jnp.stack([got[0], got[2]]).astype(F32)

    def reduce_first(c, wait=(), behind=()):
        got = after(permute(after(c.away, *wait), x_second), *behind)
        c.away = (c.here[1] + got[1].astype(F32)).astype(BF)
        c.here = (c.here[0], got[0])

    def reduce_second(c, wait=(), behind=()):
        got = after(permute(after(c.away, *wait), x_first), *behind)
        here, first_got = c.here
        c.total = (here + first_got.astype(F32) + got.astype(F32)).astype(BF).reshape(8, t, d)

    def reduce_last(c, *wait):
        total = after(c.total, *wait) if wait else c.total
        c.blocks = lax.all_to_all(total, Z, 0, 0, tiled=True)
        c.input_grad = jnp.sum(c.blocks.astype(F32), 0).astype(BF)

    def weights(c, *wait):
        grads = after(c.grad_all, *wait).reshape(64 * t, f)
        return lax.dot_general(c.tokens, grads, (((0,), (0,)), ((), ())), preferred_element_type=F32)

    a, b = Chunk(), Chunk()
    spread(a, inputs[:t])
    along_x(a)
    spread(b, inputs[t:], a.own)
    assemble(a)
    along_x(b, a.three)
    project(a)
    sum_first(a)
    sum_second(a)
    assemble(b)
    project(b, a.theirs)
    gelu(a, cotangents[0])
    spread_first(a)
    sum_first(b)
    spread_second(a, wait=(b.send,))
    sum_second(b)
    back(a)
    gelu(b, cotangents[1], a.away)
    spread_first(b)
    reduce_first(a, behind=(b.grad,))
    reduce_second(a)
    spread_second(b, behind=(a.away,))
    back(b)
    sent = b.away
    reduce_first(b, behind=(a.total,))
    reduce_last(a, sent)
    reduce_second(b, behind=(a.blocks,))
    reduce_last(b)
    weight_grad = (weights(a, b.total) + weights(b, b.total)).astype(BF)

    input_grad = jnp.concatenate([a.input_grad, b.input_grad], 0)
    activated = jnp.stack([after(a.activated, b.total), b.activated]).reshape(CHUNKS, 8, 2, t, f)
    activated = jnp.transpose(activated, (2, 1, 0, 3, 4)).reshape(out_grad.shape)
    return activated, input_grad, weight_grad


def solution(mesh):
    fine = Mesh(mesh.devices.reshape(SIZES), AXES)
    tokens = ("zl", "zh", "x", "core")
    specs = (P(tokens, "y"), P("y", tokens), P("y", tokens))
    return jax.shard_map(
        body, mesh=fine, in_specs=specs, out_specs=(specs[1], specs[0], specs[1]), check_vma=False
    )
```

```python
import functools
import math

import jax
import jax.numpy as jnp
import numpy as np
from jax import lax
from jax.experimental import pallas as pl
from jax.experimental.pallas import tpu as pltpu
from jax.sharding import Mesh
from jax.sharding import PartitionSpec as P

gelu_coef = 0.044715

AXES = ("y", "zl", "zh", "x", "core")
SIZES = (4, 2, 4, 4, 2)
Z = ("zl", "zh")
BF = jnp.bfloat16
F32 = jnp.float32


def permute(array, move):
    pairs = []
    for y, zl, zh, x, core in np.ndindex(*SIZES):
        y2, x2, core2 = move(y, x, core)
        source = np.ravel_multi_index((y, zl, zh, x, core), SIZES)
        target = np.ravel_multi_index((y2, zl, zh, x2, core2), SIZES)
        pairs.append((int(source), int(target)))
    return lax.ppermute(array, AXES, pairs)


first = lambda core: 3 if core else 1
second = lambda core: 1 if core else 3
swap_core = lambda y, x, core: (y, x, 1 - core)
x_first = lambda y, x, core: (y, x ^ first(core), core)
x_second = lambda y, x, core: (y, x ^ second(core), core)
y_first = lambda y, x, core: (y ^ first(core), x, core)
y_second = lambda y, x, core: (y ^ second(core), x, core)


def gelu_pair(pre, cotangent):
    scale = math.sqrt(2.0 / math.pi)
    inner = scale * (pre + gelu_coef * pre * pre * pre)
    tanh_val = jnp.tanh(inner)
    activated = (0.5 * pre * (1.0 + tanh_val)).astype(BF)
    slope = 0.5 * (1.0 + tanh_val) + 0.5 * pre * (1.0 - tanh_val * tanh_val) * scale * (
        1.0 + 3.0 * gelu_coef * pre * pre
    )
    return activated, (cotangent.astype(F32) * slope).astype(BF)


def gelu_kernel(place_ref, own_ref, other_ref, cot_ref, act_ref, grad_ref):
    for slot in range(own_ref.shape[0]):
        pre = own_ref[slot] + other_ref[slot].astype(F32)
        activated, grad = gelu_pair(pre, cot_ref[place_ref[slot]])
        act_ref[place_ref[slot]] = activated
        grad_ref[slot] = grad


def gelu_call(place, own, other, cotangent):
    whole = pl.BlockSpec(memory_space=pltpu.VMEM)
    return pl.pallas_call(
        gelu_kernel,
        in_specs=[pl.BlockSpec(memory_space=pltpu.SMEM), whole, whole, whole],
        out_specs=[whole, whole],
        out_shape=[jax.ShapeDtypeStruct(own.shape, BF)] * 2,
        compiler_params=pltpu.CompilerParams(vmem_limit_bytes=16 * 2**20),
        cost_estimate=pl.CostEstimate(flops=30 * own.size, bytes_accessed=12 * own.size, transcendentals=own.size),
        name="gelu",
    )(place, own, other, cotangent)


def order_kernel(place_ref, a_ref, b_ref, c_ref, out_ref):
    out_ref[:, pl.ds(place_ref[0], 1)] = a_ref[...][:, None]
    out_ref[:, pl.ds(place_ref[1], 1)] = b_ref[...][:, None]
    out_ref[:, pl.ds(place_ref[2], 1)] = c_ref[0][:, None]
    out_ref[:, pl.ds(place_ref[3], 1)] = c_ref[1][:, None]


def order_call(place, a, b, c):
    slots, rows, f = a.shape
    whole = pl.BlockSpec(memory_space=pltpu.VMEM)
    return pl.pallas_call(
        order_kernel,
        in_specs=[pl.BlockSpec(memory_space=pltpu.SMEM), whole, whole, whole],
        out_specs=whole,
        out_shape=jax.ShapeDtypeStruct((slots, 4, rows, f), BF),
        compiler_params=pltpu.CompilerParams(vmem_limit_bytes=16 * 2**20),
        cost_estimate=pl.CostEstimate(flops=0, bytes_accessed=16 * a.size, transcendentals=0),
        name="order",
    )(place, a, b, c)


CHUNKS = 2


def copy_kernel(block_ref, *copies_refs):
    for i, copies_ref in enumerate(copies_refs):
        copies_ref[...] = jnp.broadcast_to(block_ref[i][None], copies_ref.shape)


def copy_call(blocks):
    chunks, t, d = blocks.shape
    whole = pl.BlockSpec(memory_space=pltpu.VMEM)
    return pl.pallas_call(
        copy_kernel,
        in_specs=[whole],
        out_specs=[whole] * chunks,
        out_shape=[jax.ShapeDtypeStruct((8, t, d), BF)] * chunks,
        compiler_params=pltpu.CompilerParams(vmem_limit_bytes=16 * 2**20),
        name="copies",
    )(blocks)


def after(value, *others):
    return lax.optimization_barrier((value, *others))[0] if others else value


class Chunk:
    pass


def body(inputs, weight, out_grad):
    y, x, core = lax.axis_index("y"), lax.axis_index("x"), lax.axis_index("core")
    d, f = weight.shape
    t = inputs.shape[0] // CHUNKS
    near = jnp.where(core == 0, 1, 3)
    far = jnp.where(core == 0, 3, 1)
    pick = lambda a, i: lax.dynamic_index_in_dim(a, i, 1, keepdims=False)

    steps = jnp.stack([jnp.int32(0), near, far, jnp.int32(2), jnp.int32(0), far, near, jnp.int32(2)]).astype(jnp.int32)
    place = ((x ^ steps) * 2 + (core ^ (jnp.arange(8, dtype=jnp.int32) // 4))).astype(jnp.int32)
    order = jnp.stack([y, y ^ far, y ^ near, y ^ 2]).astype(jnp.int32)
    cotangents = jnp.transpose(out_grad.reshape(2, 8, CHUNKS, t, f), (2, 1, 0, 3, 4)).reshape(CHUNKS, 8, 2 * t, f)

    def spread(c, copies, *wait):
        copies = after(copies, *wait)
        c.own = lax.all_to_all(copies, Z, 0, 0, tiled=True)

    def along_x(c, *wait):
        source = after(c.own, *wait) if wait else c.own
        c.one = permute(source, x_first)
        c.two = permute(source, x_second)
        c.three = permute(c.one, x_second)

    def assemble(c):
        c.other = [permute(p, swap_core) for p in (c.own, c.one, c.two, c.three)]
        c.tokens = jnp.concatenate([c.own, c.one, c.two, c.three] + c.other, 0).reshape(64 * t, d)

    def project(c, *wait):
        tokens = after(c.tokens, *wait) if wait else c.tokens
        c.part = jnp.dot(tokens, weight, preferred_element_type=F32).reshape(8, 4, 2 * t, f)
        c.send = jnp.stack([pick(c.part, y ^ near), pick(c.part, y ^ 2)]).astype(BF)

    def sum_first(c):
        got = permute(c.send, y_first).astype(F32)
        c.mine = pick(c.part, y) + got[0]
        c.theirs = (pick(c.part, y ^ far) + got[1]).astype(BF)

    def sum_second(c):
        c.got = permute(c.theirs, y_second)

    def gelu(c, cotangent, *wait):
        got = after(c.got, *wait) if wait else c.got
        c.activated, c.grad = gelu_call(place, c.mine, got, cotangent)

    def spread_first(c):
        c.grad_far = permute(c.grad, y_second)

    def spread_second(c, wait=(), behind=()):
        rest = permute(after(jnp.stack([c.grad, c.grad_far]), *wait), y_first)
        c.grad_all = order_call(order, c.grad, c.grad_far, after(rest, *behind)).reshape(2, 32 * t, f)

    def back(c, *wait):
        dims = (((1,), (1,)), ((), ()))
        give = lax.dot_general(c.grad_all[1], weight, dims, preferred_element_type=F32).astype(BF)
        keep = lax.dot_general(after(c.grad_all[0], *wait), weight, dims, preferred_element_type=F32).reshape(4, 8 * t, d)
        got = permute(give.reshape(4, 8 * t, d), swap_core)
        c.away = (keep[2:] + got[2:].astype(F32)).astype(BF)
        c.here = keep[:2] + got[:2].astype(F32)

    def reduce_first(c, wait=(), behind=()):
        got = after(permute(after(c.away, *wait), x_second), *behind)
        c.away = (c.here[1] + got[1].astype(F32)).astype(BF)
        c.here = (c.here[0], got[0])

    def reduce_second(c, wait=(), behind=()):
        got = after(permute(after(c.away, *wait), x_first), *behind)
        here, first_got = c.here
        c.total = (here + first_got.astype(F32) + got.astype(F32)).astype(BF).reshape(8, t, d)

    def reduce_last(c, *wait):
        total = after(c.total, *wait) if wait else c.total
        c.blocks = lax.all_to_all(total, Z, 0, 0, tiled=True)
        c.input_grad = jnp.sum(c.blocks.astype(F32), 0).astype(BF)

    def weights(c, *wait):
        grads = after(c.grad_all, *wait).reshape(64 * t, f)
        return lax.dot_general(c.tokens, grads, (((0,), (0,)), ((), ())), preferred_element_type=F32)

    a, b = Chunk(), Chunk()
    copies = copy_call(inputs.reshape(CHUNKS, t, d))
    spread(a, copies[0])
    along_x(a)
    spread(b, copies[1], a.own)
    assemble(a)
    along_x(b, a.three)
    project(a)
    sum_first(a)
    sum_second(a)
    assemble(b)
    project(b, a.theirs)
    gelu(a, cotangents[0])
    spread_first(a)
    sum_first(b)
    spread_second(a, wait=(b.send,))
    sum_second(b)
    back(a, b.theirs)
    gelu(b, cotangents[1], a.away)
    spread_first(b)
    reduce_first(a, behind=(b.grad,))
    reduce_second(a)
    spread_second(b, behind=(a.away,))
    back(b)
    sent = b.away
    reduce_first(b, behind=(a.total,))
    reduce_last(a, sent)
    reduce_second(b, behind=(a.blocks,))
    reduce_last(b)
    weight_grad = (weights(a, b.total) + weights(b, b.total)).astype(BF)

    input_grad = jnp.concatenate([a.input_grad, b.input_grad], 0)
    activated = jnp.stack([after(a.activated, b.total), b.activated]).reshape(CHUNKS, 8, 2, t, f)
    activated = jnp.transpose(activated, (2, 1, 0, 3, 4)).reshape(out_grad.shape)
    return activated, input_grad, weight_grad


def solution(mesh):
    fine = Mesh(mesh.devices.reshape(SIZES), AXES)
    tokens = ("zl", "zh", "x", "core")
    specs = (P(tokens, "y"), P("y", tokens), P("y", tokens))
    return jax.shard_map(
        body, mesh=fine, in_specs=specs, out_specs=(specs[1], specs[0], specs[1]), check_vma=False
    )
```

```python
import functools
import math

import jax
import jax.numpy as jnp
import numpy as np
from jax import lax
from jax.experimental import pallas as pl
from jax.experimental.pallas import tpu as pltpu
from jax.sharding import Mesh
from jax.sharding import PartitionSpec as P

gelu_coef = 0.044715

AXES = ("y", "zl", "zh", "x", "core")
SIZES = (4, 2, 4, 4, 2)
Z = ("zl", "zh")
BF = jnp.bfloat16
F32 = jnp.float32


def permute(array, move):
    pairs = []
    for y, zl, zh, x, core in np.ndindex(*SIZES):
        y2, x2, core2 = move(y, x, core)
        source = np.ravel_multi_index((y, zl, zh, x, core), SIZES)
        target = np.ravel_multi_index((y2, zl, zh, x2, core2), SIZES)
        pairs.append((int(source), int(target)))
    return lax.ppermute(array, AXES, pairs)


first = lambda core: 3 if core else 1
second = lambda core: 1 if core else 3
swap_core = lambda y, x, core: (y, x, 1 - core)
x_first = lambda y, x, core: (y, x ^ first(core), core)
x_second = lambda y, x, core: (y, x ^ second(core), core)
y_first = lambda y, x, core: (y ^ first(core), x, core)
y_second = lambda y, x, core: (y ^ second(core), x, core)


def gelu_pair(pre, cotangent):
    scale = math.sqrt(2.0 / math.pi)
    inner = scale * (pre + gelu_coef * pre * pre * pre)
    tanh_val = jnp.tanh(inner)
    activated = (0.5 * pre * (1.0 + tanh_val)).astype(BF)
    slope = 0.5 * (1.0 + tanh_val) + 0.5 * pre * (1.0 - tanh_val * tanh_val) * scale * (
        1.0 + 3.0 * gelu_coef * pre * pre
    )
    return activated, (cotangent.astype(F32) * slope).astype(BF)


def gelu_kernel(place_ref, own_ref, other_ref, cot_ref, act_ref, grad_ref):
    for slot in range(own_ref.shape[0]):
        pre = own_ref[slot] + other_ref[slot].astype(F32)
        activated, grad = gelu_pair(pre, cot_ref[place_ref[slot]])
        act_ref[place_ref[slot]] = activated
        grad_ref[slot] = grad


def gelu_call(place, own, other, cotangent):
    whole = pl.BlockSpec(memory_space=pltpu.VMEM)
    return pl.pallas_call(
        gelu_kernel,
        in_specs=[pl.BlockSpec(memory_space=pltpu.SMEM), whole, whole, whole],
        out_specs=[whole, whole],
        out_shape=[jax.ShapeDtypeStruct(own.shape, BF)] * 2,
        compiler_params=pltpu.CompilerParams(vmem_limit_bytes=16 * 2**20),
        cost_estimate=pl.CostEstimate(flops=30 * own.size, bytes_accessed=12 * own.size, transcendentals=own.size),
        name="gelu",
    )(place, own, other, cotangent)


def order_kernel(place_ref, a_ref, b_ref, c_ref, out_ref):
    out_ref[:, pl.ds(place_ref[0], 1)] = a_ref[...][:, None]
    out_ref[:, pl.ds(place_ref[1], 1)] = b_ref[...][:, None]
    out_ref[:, pl.ds(place_ref[2], 1)] = c_ref[0][:, None]
    out_ref[:, pl.ds(place_ref[3], 1)] = c_ref[1][:, None]


def order_call(place, a, b, c):
    slots, rows, f = a.shape
    whole = pl.BlockSpec(memory_space=pltpu.VMEM)
    return pl.pallas_call(
        order_kernel,
        in_specs=[pl.BlockSpec(memory_space=pltpu.SMEM), whole, whole, whole],
        out_specs=whole,
        out_shape=jax.ShapeDtypeStruct((slots, 4, rows, f), BF),
        compiler_params=pltpu.CompilerParams(vmem_limit_bytes=16 * 2**20),
        cost_estimate=pl.CostEstimate(flops=0, bytes_accessed=16 * a.size, transcendentals=0),
        name="order",
    )(place, a, b, c)


CHUNKS = 2


def copy_kernel(block_ref, *copies_refs):
    for i, copies_ref in enumerate(copies_refs):
        copies_ref[...] = jnp.broadcast_to(block_ref[i][None], copies_ref.shape)


def copy_call(blocks):
    chunks, t, d = blocks.shape
    whole = pl.BlockSpec(memory_space=pltpu.VMEM)
    return pl.pallas_call(
        copy_kernel,
        in_specs=[whole],
        out_specs=[whole] * chunks,
        out_shape=[jax.ShapeDtypeStruct((8, t, d), BF)] * chunks,
        compiler_params=pltpu.CompilerParams(vmem_limit_bytes=16 * 2**20),
        name="copies",
    )(blocks)


def after(value, *others):
    return lax.optimization_barrier((value, *others))[0] if others else value


class Chunk:
    pass


def body(inputs, weight, out_grad):
    y, x, core = lax.axis_index("y"), lax.axis_index("x"), lax.axis_index("core")
    d, f = weight.shape
    t = inputs.shape[0] // CHUNKS
    near = jnp.where(core == 0, 1, 3)
    far = jnp.where(core == 0, 3, 1)
    pick = lambda a, i: lax.dynamic_index_in_dim(a, i, 1, keepdims=False)

    steps = jnp.stack([jnp.int32(0), near, far, jnp.int32(2)]).astype(jnp.int32)
    place = ((x ^ steps)[None] * 2 + (core ^ jnp.arange(2, dtype=jnp.int32))[:, None]).reshape(8).astype(jnp.int32)
    order = jnp.stack([y, y ^ far, y ^ near, y ^ 2]).astype(jnp.int32)
    cotangents = jnp.transpose(out_grad.reshape(2, 8, CHUNKS, t, f), (2, 1, 0, 3, 4)).reshape(CHUNKS, 8, 2 * t, f)

    def spread(c, copies, *wait):
        copies = after(copies, *wait)
        c.own = lax.all_to_all(copies, Z, 0, 0, tiled=True)

    def along_x(c, *wait):
        source = after(c.own, *wait) if wait else c.own
        c.one = permute(source, x_first)
        c.two = permute(source, x_second)
        c.three = permute(c.one, x_second)

    def assemble(c):
        c.other = [permute(p, swap_core) for p in (c.own, c.two, c.one, c.three)]
        c.tokens = jnp.concatenate([c.own, c.one, c.two, c.three] + c.other, 0).reshape(64 * t, d)

    def project(c, *wait):
        tokens = after(c.tokens, *wait) if wait else c.tokens
        c.part = jnp.dot(tokens, weight, preferred_element_type=F32).reshape(8, 4, 2 * t, f)
        c.send = jnp.stack([pick(c.part, y ^ near), pick(c.part, y ^ 2)]).astype(BF)

    def sum_first(c):
        got = permute(c.send, y_first).astype(F32)
        c.mine = pick(c.part, y) + got[0]
        c.theirs = (pick(c.part, y ^ far) + got[1]).astype(BF)

    def sum_second(c):
        c.got = permute(c.theirs, y_second)

    def gelu(c, cotangent, *wait):
        got = after(c.got, *wait) if wait else c.got
        c.activated, c.grad = gelu_call(place, c.mine, got, cotangent)

    def spread_first(c):
        c.grad_far = permute(c.grad, y_second)

    def spread_second(c, wait=(), behind=()):
        rest = permute(after(jnp.stack([c.grad, c.grad_far]), *wait), y_first)
        c.grad_all = order_call(order, c.grad, c.grad_far, after(rest, *behind)).reshape(2, 32 * t, f)

    def back(c, *wait):
        dims = (((1,), (1,)), ((), ()))
        give = lax.dot_general(c.grad_all[1], weight, dims, preferred_element_type=F32).astype(BF)
        keep = lax.dot_general(c.grad_all[0], weight, dims, preferred_element_type=F32).reshape(4, 8 * t, d)
        got = permute(give.reshape(4, 8 * t, d), swap_core)
        c.away = (keep[2:] + jnp.stack([got[1], got[3]]).astype(F32)).astype(BF)
        c.here = keep[:2] + jnp.stack([got[0], got[2]]).astype(F32)

    def reduce_first(c, wait=(), behind=()):
        got = after(permute(after(c.away, *wait), x_second), *behind)
        c.away = (c.here[1] + got[1].astype(F32)).astype(BF)
        c.here = (c.here[0], got[0])

    def reduce_second(c, wait=(), behind=()):
        got = after(permute(after(c.away, *wait), x_first), *behind)
        here, first_got = c.here
        c.total = (here + first_got.astype(F32) + got.astype(F32)).astype(BF).reshape(8, t, d)

    def reduce_last(c, *wait):
        total = after(c.total, *wait) if wait else c.total
        c.blocks = lax.all_to_all(total, Z, 0, 0, tiled=True)
        c.input_grad = jnp.sum(c.blocks.astype(F32), 0).astype(BF)

    def weights(c, *wait):
        grads = after(c.grad_all, *wait).reshape(64 * t, f)
        return lax.dot_general(c.tokens, grads, (((0,), (0,)), ((), ())), preferred_element_type=F32)

    a, b = Chunk(), Chunk()
    copies = copy_call(inputs.reshape(CHUNKS, t, d))
    spread(a, copies[0])
    along_x(a)
    spread(b, copies[1], a.own)
    assemble(a)
    along_x(b, a.three)
    project(a)
    sum_first(a)
    sum_second(a)
    assemble(b)
    project(b, a.theirs)
    gelu(a, cotangents[0])
    spread_first(a)
    sum_first(b)
    spread_second(a, wait=(b.send,))
    sum_second(b)
    back(a)
    gelu(b, cotangents[1], a.away)
    spread_first(b)
    reduce_first(a, behind=(b.grad,))
    reduce_second(a)
    spread_second(b, behind=(a.away,))
    back(b)
    sent = b.away
    reduce_first(b, behind=(a.total,))
    reduce_last(a, sent)
    reduce_second(b, behind=(a.blocks,))
    reduce_last(b)
    weight_grad = (weights(a, b.total) + weights(b, b.total)).astype(BF)

    input_grad = jnp.concatenate([a.input_grad, b.input_grad], 0)
    activated = jnp.stack([after(a.activated, b.total), b.activated]).reshape(CHUNKS, 8, 2, t, f)
    activated = jnp.transpose(activated, (2, 1, 0, 3, 4)).reshape(out_grad.shape)
    return activated, input_grad, weight_grad


def solution(mesh):
    fine = Mesh(mesh.devices.reshape(SIZES), AXES)
    tokens = ("zl", "zh", "x", "core")
    specs = (P(tokens, "y"), P("y", tokens), P("y", tokens))
    return jax.shard_map(
        body, mesh=fine, in_specs=specs, out_specs=(specs[1], specs[0], specs[1]), check_vma=False
    )
```
